32 devices in a mesh: parts: 2 (over x), col: 16 (over z, y, core).
Axes of the slice: x: 2, y: 2, z: 4, core: 2. Of those that a mesh axis runs over, the one named last changes fastest.
Arguments:
- view_factors: bfloat16 [8192, 4096], P(('parts', 'col')), parts along dimension 0, may hold values from -0.09375 to 0.09375
- direct_coeff: bfloat16 [8192, 2304], P(('parts', 'col')), parts along dimension 0, may hold values from -6 to 6
- material: int32 [8192], P(('parts', 'col')), parts along dimension 0, may hold values from 0 to 15
- albedo: float32 [32], P('parts'), parts along dimension 0, may hold values from 0.1 to 0.9
- sky_matrix: bfloat16 [2304, 128], P('col'), may hold values from -0.125 to 0.125
- sky_order: int32 [2304], replicated, may hold values from 0 to 2303, each once
Outputs:
- irradiance: bfloat16 [8192, 128], P(('parts', 'col')), parts along dimension 0
The draws below stay inside these ranges and needn't reach their ends.
There are 2 independent parts, one for each index of `parts`. The reference program is written for one: setup_inputs(seed, part) draws one part's arguments, and reference() takes and returns one part's arrays. A program takes and returns all parts, laid end to end along the dimension named above; an argument that names none is the same for every part. Nothing has to cross between parts.
Inputs may be any that keep to these rules, and one draw needn't show every extreme that they name: sky_order names each of 0 to 2303 once.
All inputs are finite; a program needn't handle non-finite values.
Results may differ from the reference program's by a relative error of at most 0.0055.
Values may be sent and summed in bfloat16 or wider, within the bound.
No kernel may reach another device: no remote copies, remote signals or barrier semaphores. Data moves between devices by JAX's collectives and lax.ppermute only.
A program may use at most 128 MiB of HBM per device.

```python
import jax
import jax.numpy as jnp
from jax import lax

SKY = 2304
MATERIALS = 16
HOURS = 128
PATCHES = 4096


def set_ends(values, stream_key, smallest, largest):
    longest = values.shape.index(max(values.shape))
    spots = []
    for shift in (0, 1):
        where = [jax.random.randint(jax.random.fold_in(stream_key, axis), (), 0, length) for axis, length in enumerate(values.shape)]
        where[longest] = (where[longest] + shift) % values.shape[longest]
        spots.append(tuple(where))
    return values.at[spots[0]].set(smallest).at[spots[1]].set(largest)


def block_levels(rng, extent, cuts, least, largest):
    loudness = 1.0
    for dim, blocks in cuts:
        heights = jax.random.uniform(jax.random.fold_in(jax.random.fold_in(rng, 6), dim), (blocks,), jnp.float32, least / len(cuts), largest / len(cuts))
        loudness = loudness * jnp.repeat(jnp.exp(heights), extent[dim] // blocks).reshape((-1,) + (1,) * (len(extent) - 1 - dim))
    return loudness


def gaussian(rng, extent, width, bound, cuts=(), held_as=jnp.bfloat16):
    factor_of = block_levels(rng, extent, cuts, -0.22, 0.18) if cuts else 1.0
    result = jax.random.normal(rng, extent, jnp.float32) * width * factor_of
    return jnp.minimum(jnp.maximum(result, -bound), bound).astype(held_as)


def setup_inputs(seed: int = 0, part: int = 0) -> dict:
    seeds = jax.random.split(jax.random.key(seed), 7)
    part_keys = jax.random.split(jax.random.fold_in(seeds[6], part), 7)
    return {
        "view_factors": gaussian(part_keys[0], (PATCHES, PATCHES), PATCHES ** -0.5, 0.09375, ((0, 16),)),
        "direct_coeff": gaussian(part_keys[1], (PATCHES, SKY), 1.0, 6.0, ((0, 16),)),
        "material": set_ends(jax.random.randint(part_keys[2], (PATCHES,), 0, MATERIALS), jax.random.fold_in(part_keys[2], 1), 0, MATERIALS - 1).astype(jnp.int32),
        "albedo": jnp.clip(jax.random.uniform(part_keys[3], (MATERIALS,), jnp.float32, 0.1, 0.9), 0.1, 0.9),
        "sky_matrix": gaussian(seeds[4], (SKY, HOURS), SKY ** -0.5, 0.125, ((0, 16),)),
        "sky_order": jax.random.permutation(seeds[5], SKY).astype(jnp.int32),
    }


def reference(view_factors, direct_coeff, material, albedo, sky_matrix, sky_order):
    reflectance = albedo[material]
    reflected = (reflectance[:, None] * direct_coeff.astype(jnp.float32)).astype(jnp.bfloat16)
    bounce = jnp.dot(view_factors, reflected, preferred_element_type=jnp.float32)
    coefficients = direct_coeff.astype(jnp.float32) + bounce
    ordered = sky_matrix[sky_order.astype(jnp.int32)]
    irradiance = jnp.dot(coefficients, ordered.astype(jnp.float32), precision=lax.Precision.HIGHEST)
    return irradiance.astype(jnp.bfloat16)
```

```python
import jax
import jax.numpy as jnp
from jax import lax
from jax.sharding import PartitionSpec as P


def exchange_plan(size):
    bits = [1 << b for b in range(1, size.bit_length() - 1)][::-1]
    return bits, bits[-1:] + bits[:-1]


def arrival(order):
    masks = [0]
    for bit in order:
        masks = masks + [m ^ bit for m in masks]
    return masks


def owners(size):
    even, odd = (arrival(order) for order in exchange_plan(size))
    return even + [m ^ 1 for m in odd], odd + [m ^ 1 for m in even]


def gather(block, size):
    for even, odd in zip(*exchange_plan(size)):
        pairs = [(i, i ^ (odd if i & 1 else even)) for i in range(size)]
        block = jnp.concatenate([block, lax.ppermute(block, "col", pairs)], axis=0)
    other = lax.ppermute(block, "col", [(i, i ^ 1) for i in range(size)])
    return jnp.concatenate([block, other], axis=0)


def shards(size, view_factors, direct_coeff, material, albedo, sky_matrix, sky_order):
    me = lax.axis_index("col")
    even, odd = owners(size)
    masks = jnp.where(me & 1 == 0, jnp.array(even, jnp.int32), jnp.array(odd, jnp.int32))
    owner = me ^ masks
    rows = sky_matrix.shape[0]
    patches = direct_coeff.shape[0]
    held = (owner[:, None] * rows + jnp.arange(rows, dtype=jnp.int32)[None, :]).reshape(-1)
    matches = material[:, None] == jnp.arange(albedo.shape[0], dtype=jnp.int32)[None, :]
    reflectance = jnp.sum(jnp.where(matches, albedo[None, :], 0.0), axis=1)
    place = (sky_order[:, None] == held[None, :]).astype(jnp.bfloat16)
    direct = jnp.dot(direct_coeff, place, preferred_element_type=jnp.float32).astype(jnp.bfloat16)
    reflected = (reflectance[:, None] * direct.astype(jnp.float32)).astype(jnp.bfloat16)
    sky = gather(sky_matrix, size)
    hours = jnp.dot(reflected, sky, preferred_element_type=jnp.float32).astype(jnp.bfloat16)
    direct_hours = jnp.dot(direct, sky, preferred_element_type=jnp.float32)
    all_hours = gather(hours, size)
    total = direct_hours
    for slot in range(size):
        columns = lax.dynamic_slice_in_dim(view_factors, owner[slot] * patches, patches, axis=1)
        total += jnp.dot(columns, all_hours[slot * patches : (slot + 1) * patches], preferred_element_type=jnp.float32)
    return total.astype(jnp.bfloat16)


def solution(mesh):
    size = mesh.shape["col"]

    def body(*args):
        return shards(size, *args)

    return jax.shard_map(
        body,
        mesh=mesh,
        in_specs=(
            P(("parts", "col"), None),
            P(("parts", "col"), None),
            P(("parts", "col")),
            P("parts"),
            P("col", None),
            P(),
        ),
        out_specs=P(("parts", "col"), None),
        check_vma=False,
    )
```

```python
import functools

import jax
import jax.numpy as jnp
from jax import lax
from jax.experimental import pallas as pl
from jax.experimental.pallas import tpu as pltpu
from jax.sharding import PartitionSpec as P

WHOLE = pl.BlockSpec(memory_space=pltpu.VMEM)
ANYWHERE = pl.BlockSpec(memory_space=pltpu.HBM)
SCALARS = pl.BlockSpec(memory_space=pltpu.SMEM)


def exchange_plan(size):
    bits = [1 << b for b in range(1, size.bit_length() - 1)][::-1]
    return bits[:-2] + bits[-2:][::-1], bits


def arrival(order):
    masks = [0]
    for bit in order:
        masks = masks + [m ^ bit for m in masks]
    return masks


def owner_of(me, even, odd):
    return me ^ jnp.where(me & 1 == 0, even, odd)


def call(kernel, name, outs, specs, flops, *args, scratch=(), vmem=24):
    return pl.pallas_call(
        kernel,
        scratch_shapes=scratch,
        out_shape=outs,
        in_specs=specs,
        out_specs=jax.tree.map(lambda _: WHOLE, outs),
        compiler_params=pltpu.CompilerParams(vmem_limit_bytes=vmem * 2**20),
        cost_estimate=pl.CostEstimate(flops=flops, bytes_accessed=0, transcendentals=0),
        name=name,
    )(*args)


def prepare_kernel(size, albedo_in, material_in, order_in, sky_in, direct_in, me_ref, *refs):
    sky_out, direct_out, reflectance_out, place_out, albedo_ref, material_ref, order_ref, sems = refs
    moves = ((albedo_in, albedo_ref), (material_in, material_ref), (order_in, order_ref))
    moves += ((sky_in, sky_out), (direct_in, direct_out))
    copies = [pltpu.make_async_copy(source, target, sems.at[i]) for i, (source, target) in enumerate(moves)]
    for copy in copies:
        copy.start()
    for copy in copies[:3]:
        copy.wait()
    material = material_ref[...].reshape(1, -1)
    reflectance = jnp.zeros(material.shape, jnp.float32)
    for m in range(albedo_ref.shape[0]):
        reflectance = jnp.where(material == m, albedo_ref[m], reflectance)
    reflectance_out[...] = jnp.broadcast_to(reflectance, (128, reflectance.shape[1])).T
    me = me_ref[0]
    rows = sky_in.shape[0]
    order = order_ref[...].reshape(1, -1)
    owner = (order * -(-(1 << 20) // rows)) >> 20
    row = order - owner * rows
    apart = owner ^ me
    slot = jnp.where(apart & 1 != 0, size // 2, 0)
    for k, (even, odd) in enumerate(zip(*exchange_plan(size))):
        slot += jnp.where(apart & jnp.where(owner & 1 == 0, even, odd) != 0, 1 << k, 0)
    place_out[...] = slot * rows + row
    for copy in copies[3:]:
        copy.wait()


def permute_kernel(start, place_ref, reflectance_ref, direct_ref, sorted_ref, reflected_ref):
    count = sorted_ref.shape[1]
    place = place_ref[...]
    reflectance = reflectance_ref[:, :1]
    step = 384
    for j in range(0, count, step):
        width = min(step, count - j)
        position = lax.broadcasted_iota(jnp.int32, (width, place.shape[1]), 0) + (start + j)
        pick = jnp.where(position == place, 1.0, 0.0).astype(jnp.bfloat16)
        part = lax.dot_general(direct_ref[...], pick, (((1,), (1,)), ((), ())), preferred_element_type=jnp.float32)
        sorted_ref[:, j : j + width] = part.astype(jnp.bfloat16)
        reflected_ref[:, j : j + width] = (reflectance * part).astype(jnp.bfloat16)


def dot_kernel(a_ref, b_ref, out_ref):
    out_ref[...] = jnp.dot(a_ref[...], b_ref[...], preferred_element_type=jnp.float32)


def direct_kernel(own_ref, other_ref, sky_own_ref, sky_other_ref, factors_ref, out_ref, factors_out, sem):
    copy = pltpu.make_async_copy(factors_ref, factors_out, sem)
    copy.start()
    out = jnp.dot(own_ref[...], sky_own_ref[...], preferred_element_type=jnp.float32)
    out_ref[...] = out + jnp.dot(other_ref[...], sky_other_ref[...], preferred_element_type=jnp.float32)
    copy.wait()


def add_dot_kernel(base_ref, a_ref, b_ref, out_ref):
    part = jnp.dot(a_ref[...], b_ref[...], preferred_element_type=jnp.float32)
    out_ref[...] = (base_ref[...] + part).astype(out_ref.dtype)


def bounce_kernel(masks, me_ref, base_ref, factors_ref, hours_ref, out_ref):
    me = me_ref[0]
    total = base_ref[...]
    patches = out_ref.shape[0]
    for slot, (even, odd) in enumerate(masks):
        first = pl.multiple_of(owner_of(me, even, odd) * patches, patches)
        total += jnp.dot(
            factors_ref[:, pl.ds(first, patches)],
            hours_ref[slot * patches : (slot + 1) * patches, :],
            preferred_element_type=jnp.float32,
        )
    out_ref[...] = total.astype(out_ref.dtype)


def shards(size, view_factors, direct_coeff, material, albedo, sky_matrix, sky_order):
    me = lax.axis_index("col")
    even, odd = exchange_plan(size)
    rows, hours = sky_matrix.shape
    patches, skies = direct_coeff.shape
    half = size // 2
    pairs = [[(i, i ^ (b if i & 1 else a)) for i in range(size)] for a, b in zip(even, odd)]
    cores = [(i, i ^ 1) for i in range(size)]

    def exchange(block, step):
        return jnp.concatenate([block, lax.ppermute(block, "col", pairs[step])], axis=0)

    span = half * rows
    index = me.reshape(1)
    sky_own, direct_coeff, reflectance, place = call(
        functools.partial(prepare_kernel, size),
        "prepare",
        (
            pltpu.VMEM(sky_matrix.shape, sky_matrix.dtype),
            pltpu.VMEM(direct_coeff.shape, direct_coeff.dtype),
            pltpu.VMEM((patches, 128), jnp.float32),
            pltpu.VMEM((1, skies), jnp.int32),
        ),
        [ANYWHERE] * 5 + [SCALARS],
        10**9,
        *(pltpu.with_memory_space_constraint(x, pltpu.HBM) for x in (albedo, material, sky_order, sky_matrix, direct_coeff)),
        index,
        scratch=[
            pltpu.SMEM(albedo.shape, albedo.dtype),
            pltpu.VMEM(material.shape, material.dtype),
            pltpu.VMEM(sky_order.shape, sky_order.dtype),
            pltpu.SemaphoreType.DMA((5,)),
        ],
    )

    def permute(h, after):
        where, _ = lax.optimization_barrier((place, after))
        return call(
            functools.partial(permute_kernel, h * span),
            f"permute{h}",
            (jax.ShapeDtypeStruct((patches, span), jnp.bfloat16),) * 2,
            [WHOLE] * 3,
            2 * patches * skies * span,
            where,
            reflectance,
            direct_coeff,
        )

    sky = sky_matrix
    split = []
    for step in range(len(even)):
        came = lax.ppermute(sky, "col", pairs[step])
        if 0 < step < 3:
            split.append(permute(step - 1, sky))
            came, split[-1] = lax.optimization_barrier((came, split[-1]))
        sky = jnp.concatenate([sky if step else sky_own, came], axis=0)
    sky_other = lax.ppermute(sky, "col", cores)

    flat = jax.ShapeDtypeStruct((patches, hours), jnp.float32)
    flops = 2 * patches * span * hours
    part = call(dot_kernel, "hours_own", flat, [WHOLE] * 2, flops, split[0][1], sky)
    own = call(
        add_dot_kernel, "hours_all", jax.ShapeDtypeStruct(flat.shape, jnp.bfloat16), [WHOLE] * 3, flops, part, split[1][1], sky_other
    )
    held = own
    for step in range(len(even)):
        came = lax.ppermute(held, "col", pairs[step])
        if step == 0:
            _, sky_own, sky_other_own = lax.optimization_barrier((held, sky, sky_other))
            direct, view_factors = call(
                direct_kernel,
                "direct",
                (flat, jax.ShapeDtypeStruct(view_factors.shape, view_factors.dtype)),
                [WHOLE] * 4 + [ANYWHERE],
                2 * flops,
                split[0][0],
                split[1][0],
                sky_own,
                sky_other_own,
                view_factors,
                scratch=[pltpu.SemaphoreType.DMA],
                vmem=24,
            )
            came, direct = lax.optimization_barrier((came, direct))
        held = jnp.concatenate([held, came], axis=0)
    held_other = lax.ppermute(held, "col", cores)
    a, b = arrival(even), arrival(odd)
    flops = 2 * patches * half * patches * hours
    specs = [SCALARS, WHOLE, WHOLE, WHOLE]
    total = call(
        functools.partial(bounce_kernel, list(zip(a, b))), "bounce_own", flat, specs, flops, index, direct, view_factors, held
    )
    return call(
        functools.partial(bounce_kernel, [(y ^ 1, x ^ 1) for x, y in zip(a, b)]),
        "bounce_all",
        jax.ShapeDtypeStruct(flat.shape, jnp.bfloat16),
        specs,
        flops,
        index,
        total,
        view_factors,
        held_other,
    )


def solution(mesh):
    return jax.shard_map(
        functools.partial(shards, mesh.shape["col"]),
        mesh=mesh,
        in_specs=(
            P(("parts", "col"), None),
            P(("parts", "col"), None),
            P(("parts", "col")),
            P("parts"),
            P("col", None),
            P(),
        ),
        out_specs=P(("parts", "col"), None),
        check_vma=False,
    )
```

```python
import functools

import jax
import jax.numpy as jnp
from jax import lax
from jax.experimental import pallas as pl
from jax.experimental.pallas import tpu as pltpu
from jax.sharding import PartitionSpec as P

WHOLE = pl.BlockSpec(memory_space=pltpu.VMEM)
ANYWHERE = pl.BlockSpec(memory_space=pltpu.HBM)
SCALARS = pl.BlockSpec(memory_space=pltpu.SMEM)


def parity(i):
    for shift in (8, 4, 2, 1):
        i = i ^ (i >> shift)
    return i & 1


class Piece:
    def __init__(self, value, masks):
        self.value = value
        self.masks = masks


def join(*pieces):
    masks = [sum((p.masks[c] for p in pieces), []) for c in range(2)]
    return Piece(None if pieces[0].value is None else jnp.concatenate([p.value for p in pieces], axis=0), masks)


def swap(size, piece, *bits):
    bits = bits * (2 // len(bits))
    pairs = [(i, i ^ bits[parity(i)]) for i in range(size)]
    masks = [[m ^ bits[c] for m in piece.masks[c ^ parity(bits[c])]] for c in range(2)]
    return Piece(None if piece.value is None else lax.ppermute(piece.value, "col", pairs), masks)


def gather(size, block, copy, early=(), late=lambda _: []):
    exchange = functools.partial(swap, size)
    near, next_, far, *farther = [2 << b | 1 for b in range(size.bit_length() - 2)]
    one, other, both = (near, next_), (next_, near), near ^ next_ ^ 1

    def wait(piece, others):
        if len(others) and piece.value is not None:
            piece.value, others = lax.optimization_barrier((piece.value, others))
        return others

    mine = [Piece(value, [[0], [0]]) for value in (block, copy)]
    for bits in farther[::-1]:
        mine = [join(piece, exchange(piece, bits)) for piece in mine]
    from_far = exchange(mine[0], far)
    came = exchange(mine[1], *one)
    ours = join(mine[1], came)
    beside = exchange(ours, *other)
    early = wait(from_far, [ours.value, *early])[1:]
    beyond = [exchange(from_far, *other), exchange(from_far, *one), exchange(from_far, both)]
    late = wait(beyond[-1], late(from_far.value))
    same = join(from_far, ours, *beyond, beside)
    return same, exchange(same, 1), early, late


def call(kernel, name, outs, specs, flops, *args, scratch=(), vmem=24):
    return pl.pallas_call(
        kernel,
        scratch_shapes=scratch,
        out_shape=outs,
        in_specs=specs,
        out_specs=jax.tree.map(lambda _: WHOLE, outs),
        compiler_params=pltpu.CompilerParams(vmem_limit_bytes=vmem * 2**20),
        cost_estimate=pl.CostEstimate(flops=flops, bytes_accessed=0, transcendentals=0),
        name=name,
    )(*args)


def prepare_kernel(albedo_in, material_in, order_in, sky_in, direct_in, me_ref, *refs):
    sky_out, direct_out, reflectance_out, where_out, albedo_ref, material_ref, order_ref, sems = refs
    moves = ((albedo_in, albedo_ref), (material_in, material_ref), (order_in, order_ref))
    moves += ((sky_in, sky_out), (direct_in, direct_out))
    copies = [pltpu.make_async_copy(source, target, sems.at[i]) for i, (source, target) in enumerate(moves)]
    for copy in copies:
        copy.start()
    for copy in copies[:3]:
        copy.wait()
    material = material_ref[...].reshape(1, -1)
    reflectance = jnp.zeros(material.shape, jnp.float32)
    for m in range(albedo_ref.shape[0]):
        reflectance = jnp.where(material == m, albedo_ref[m], reflectance)
    reflectance_out[...] = jnp.broadcast_to(reflectance, (128, reflectance.shape[1])).T
    rows = sky_in.shape[0]
    order = order_ref[...].reshape(1, -1)
    owner = (order * -(-(1 << 20) // rows)) >> 20
    where_out[:1] = owner ^ me_ref[0]
    where_out[1:] = order - owner * rows
    for copy in copies[3:]:
        copy.wait()


def permute_kernel(masks, rows, me_ref, where_ref, reflectance_ref, direct_ref, sorted_ref, reflected_ref):
    count = sorted_ref.shape[1]
    odd = parity(me_ref[0])
    apart = where_ref[:1]
    first = jnp.full(apart.shape, -count, jnp.int32)
    for slot, (mask_even, mask_odd) in enumerate(zip(*masks)):
        first = jnp.where(apart == jnp.where(odd == 0, mask_even, mask_odd), slot * rows, first)
    place = first + where_ref[1:]
    reflectance = reflectance_ref[:, :1]
    step = 384
    for j in range(0, count, step):
        width = min(step, count - j)
        position = lax.broadcasted_iota(jnp.int32, (width, place.shape[1]), 0) + j
        pick = jnp.where(position == place, 1.0, 0.0).astype(jnp.bfloat16)
        part = lax.dot_general(direct_ref[...], pick, (((1,), (1,)), ((), ())), preferred_element_type=jnp.float32)
        sorted_ref[:, j : j + width] = part.astype(jnp.bfloat16)
        reflected_ref[:, j : j + width] = (reflectance * part).astype(jnp.bfloat16)


def dot_kernel(a_ref, b_ref, out_ref):
    out_ref[...] = jnp.dot(a_ref[...], b_ref[...], preferred_element_type=jnp.float32)


def add_dot_kernel(base_ref, a_ref, b_ref, out_ref):
    part = jnp.dot(a_ref[...], b_ref[...], preferred_element_type=jnp.float32)
    out_ref[...] = (base_ref[...] + part).astype(out_ref.dtype)


def direct_kernel(first_ref, second_ref, sky_first_ref, sky_second_ref, hours_ref, out_ref, hours_out):
    hours_out[...] = hours_ref[...]
    out = jnp.dot(first_ref[...], sky_first_ref[...], preferred_element_type=jnp.float32)
    out_ref[...] = out + jnp.dot(second_ref[...], sky_second_ref[...], preferred_element_type=jnp.float32)


def bounce_kernel(masks, me_ref, base_ref, factors_ref, hours_ref, out_ref):
    me = me_ref[0]
    odd = parity(me)
    total = base_ref[...]
    patches = out_ref.shape[0]
    for slot, (mask_even, mask_odd) in enumerate(zip(*masks)):
        owner = me ^ jnp.where(odd == 0, mask_even, mask_odd)
        total += jnp.dot(
            factors_ref[:, pl.ds(pl.multiple_of(owner * patches, patches), patches)],
            hours_ref[slot * patches : (slot + 1) * patches, :],
            preferred_element_type=jnp.float32,
        )
    out_ref[...] = total.astype(out_ref.dtype)


def shards(size, view_factors, direct_coeff, material, albedo, sky_matrix, sky_order):
    index = lax.axis_index("col").reshape(1)
    rows, hours = sky_matrix.shape
    patches, skies = direct_coeff.shape
    span = size // 2 * rows
    sky, direct_coeff, reflectance, where = call(
        prepare_kernel,
        "prepare",
        (
            pltpu.VMEM(sky_matrix.shape, sky_matrix.dtype),
            pltpu.VMEM(direct_coeff.shape, direct_coeff.dtype),
            pltpu.VMEM((patches, 128), jnp.float32),
            pltpu.VMEM((2, skies), jnp.int32),
        ),
        [ANYWHERE] * 5 + [SCALARS],
        10**9,
        *(pltpu.with_memory_space_constraint(x, pltpu.HBM) for x in (albedo, material, sky_order, sky_matrix, direct_coeff)),
        index,
        scratch=[
            pltpu.SMEM(albedo.shape, albedo.dtype),
            pltpu.VMEM(material.shape, material.dtype),
            pltpu.VMEM(sky_order.shape, sky_order.dtype),
            pltpu.SemaphoreType.DMA((5,)),
        ],
    )
    same, across, _, _ = gather(size, None, None)

    def permute(piece, name, start=None):
        place = where if start is None else lax.optimization_barrier((where, start))[0]
        return call(
            functools.partial(permute_kernel, piece.masks, rows),
            name,
            (jax.ShapeDtypeStruct((patches, span), jnp.bfloat16),) * 2,
            [SCALARS] + [WHOLE] * 3,
            2 * patches * skies * span,
            index,
            place,
            reflectance,
            direct_coeff,
        )

    late = functools.partial(permute, across, "permute_across")
    same, across, first, second = gather(size, sky_matrix, sky, permute(same, "permute_same"), late)

    flat = jax.ShapeDtypeStruct((patches, hours), jnp.float32)
    short = jax.ShapeDtypeStruct((patches, hours), jnp.bfloat16)
    flops = 2 * patches * span * hours
    part = call(dot_kernel, "hours_same", flat, [WHOLE] * 2, flops, first[1], same.value)
    own = call(add_dot_kernel, "hours_all", short, [WHOLE] * 3, flops, part, second[1], across.value)
    total, copy = call(
        direct_kernel,
        "direct",
        (flat, pltpu.VMEM(own.shape, own.dtype)),
        [WHOLE] * 5,
        2 * flops,
        first[0],
        second[0],
        same.value,
        across.value,
        own,
    )
    same, across, (total,), _ = gather(size, own, copy, [total])

    def bounce(name, base, piece, out):
        return call(
            functools.partial(bounce_kernel, piece.masks),
            name,
            out,
            [SCALARS] + [WHOLE] * 3,
            2 * patches * piece.value.size,
            index,
            base,
            view_factors,
            piece.value,
        )

    return bounce("bounce_across", bounce("bounce_same", total, same, flat), across, short)


def solution(mesh):
    return jax.shard_map(
        functools.partial(shards, mesh.shape["col"]),
        mesh=mesh,
        in_specs=(
            P(("parts", "col"), None),
            P(("parts", "col"), None),
            P(("parts", "col")),
            P("parts"),
            P("col", None),
            P(),
        ),
        out_specs=P(("parts", "col"), None),
        check_vma=False,
    )
```

```python
import functools

import jax
import jax.numpy as jnp
from jax import lax
from jax.experimental import pallas as pl
from jax.experimental.pallas import tpu as pltpu
from jax.sharding import PartitionSpec as P

WHOLE = pl.BlockSpec(memory_space=pltpu.VMEM)
ANYWHERE = pl.BlockSpec(memory_space=pltpu.HBM)
SCALARS = pl.BlockSpec(memory_space=pltpu.SMEM)


def parity(i):
    for shift in (8, 4, 2, 1):
        i = i ^ (i >> shift)
    return i & 1


class Piece:
    def __init__(self, value, masks):
        self.value = value
        self.masks = masks


def join(*pieces):
    masks = [sum((p.masks[c] for p in pieces), []) for c in range(2)]
    return Piece(None if pieces[0].value is None else jnp.concatenate([p.value for p in pieces], axis=0), masks)


def swap(size, piece, *bits):
    bits = bits * (2 // len(bits))
    pairs = [(i, i ^ bits[parity(i)]) for i in range(size)]
    masks = [[m ^ bits[c] for m in piece.masks[c ^ parity(bits[c])]] for c in range(2)]
    return Piece(None if piece.value is None else lax.ppermute(piece.value, "col", pairs), masks)


def gather(size, block, copy, sent, order, early, late=None, patient=False):
    exchange = functools.partial(swap, size)
    near, next_, far, *farther = [2 << b | 1 for b in range(size.bit_length() - 2)]
    one, other, both = (near, next_), (next_, near), near ^ next_ ^ 1

    def wait(piece, values):
        if piece.value is not None:
            piece.value, values = lax.optimization_barrier((piece.value, values))
        return values

    block, copy, sent = (Piece(value, [[0], [0]]) for value in (block, copy, sent))
    for bits in farther[::-1]:
        block, copy, sent = (join(piece, exchange(piece, bits)) for piece in (block, copy, sent))
    from_far = exchange(block, far)
    ours = join(copy, exchange(sent, *one))
    beside = exchange(ours, *other)
    early, *_ = wait(from_far, [early, ours.value] if patient else [early])
    third, second, first = exchange(from_far, *other), exchange(from_far, *one), exchange(from_far, both)
    if late is not None:
        late = wait(first, late(from_far.value))
    parts = dict(ours=ours, beside=beside, far=from_far, first=first, second=second, third=third)
    gathered = join(*(parts[name] for name in order))
    gathered.head = join(*(parts[name] for name in order[:3]))
    return gathered, early, late


def call(kernel, name, outs, specs, flops, *args, scratch=(), vmem=24):
    return pl.pallas_call(
        kernel,
        scratch_shapes=scratch,
        out_shape=outs,
        in_specs=specs,
        out_specs=jax.tree.map(lambda _: WHOLE, outs),
        compiler_params=pltpu.CompilerParams(vmem_limit_bytes=vmem * 2**20),
        cost_estimate=pl.CostEstimate(flops=flops, bytes_accessed=0, transcendentals=0),
        name=name,
    )(*args)


def prepare_kernel(albedo_in, material_in, order_in, sky_in, direct_in, me_ref, *refs):
    sky_out, direct_out, reflectance_out, where_out, albedo_ref, material_ref, order_ref, sems = refs
    moves = ((albedo_in, albedo_ref), (material_in, material_ref), (order_in, order_ref))
    moves += ((sky_in, sky_out), (direct_in, direct_out))
    copies = [pltpu.make_async_copy(source, target, sems.at[i]) for i, (source, target) in enumerate(moves)]
    for copy in copies:
        copy.start()
    for copy in copies[:3]:
        copy.wait()
    material = material_ref[...].reshape(1, -1)
    reflectance = jnp.zeros(material.shape, jnp.float32)
    for m in range(albedo_ref.shape[0]):
        reflectance = jnp.where(material == m, albedo_ref[m], reflectance)
    reflectance_out[...] = jnp.broadcast_to(reflectance, (128, reflectance.shape[1])).T
    rows = sky_in.shape[0]
    order = order_ref[...].reshape(1, -1)
    owner = (order * -(-(1 << 20) // rows)) >> 20
    where_out[:1] = owner ^ me_ref[0]
    where_out[1:] = order - owner * rows
    for copy in copies[3:]:
        copy.wait()


def permute_kernel(masks, rows, me_ref, where_ref, reflectance_ref, direct_ref, sorted_ref, reflected_ref):
    count = sorted_ref.shape[1]
    odd = parity(me_ref[0])
    apart = where_ref[:1]
    first = jnp.full(apart.shape, -count, jnp.int32)
    for slot, (mask_even, mask_odd) in enumerate(zip(*masks)):
        first = jnp.where(apart == jnp.where(odd == 0, mask_even, mask_odd), slot * rows, first)
    place = first + where_ref[1:]
    reflectance = reflectance_ref[:, :1]
    step = 256
    for j in range(0, count, step):
        width = min(step, count - j)
        position = lax.broadcasted_iota(jnp.int32, (width, place.shape[1]), 0) + j
        pick = jnp.where(position == place, 1.0, 0.0).astype(jnp.bfloat16)
        part = lax.dot_general(direct_ref[...], pick, (((1,), (1,)), ((), ())), preferred_element_type=jnp.float32)
        sorted_ref[:, j : j + width] = part.astype(jnp.bfloat16)
        reflected_ref[:, j : j + width] = (reflectance * part).astype(jnp.bfloat16)


def dot_kernel(a_ref, b_ref, out_ref):
    out_ref[...] = jnp.dot(a_ref[...], b_ref[...], preferred_element_type=jnp.float32)


def add_dot_kernel(base_ref, a_ref, b_ref, out_ref):
    part = jnp.dot(a_ref[...], b_ref[...], preferred_element_type=jnp.float32)
    out_ref[...] = (base_ref[...] + part).astype(out_ref.dtype)


def copy_kernel(in_ref, out_ref):
    out_ref[...] = in_ref[...]


def direct_kernel(first_ref, second_ref, sky_first_ref, sky_second_ref, out_ref):
    out = jnp.dot(first_ref[...], sky_first_ref[...], preferred_element_type=jnp.float32)
    out_ref[...] = out + jnp.dot(second_ref[...], sky_second_ref[...], preferred_element_type=jnp.float32)


def owners(masks, me):
    odd = parity(me)
    return [me ^ jnp.where(odd == 0, mask_even, mask_odd) for mask_even, mask_odd in zip(*masks)]


def select_kernel(masks, me_ref, factors_ref, out_ref):
    patches = out_ref.shape[0]
    for slot, owner in enumerate(owners(masks, me_ref[0])):
        columns = factors_ref[:, pl.ds(pl.multiple_of(owner * patches, patches), patches)]
        out_ref[:, slot * patches : (slot + 1) * patches] = columns


def bounce_kernel(masks, me_ref, base_ref, factors_ref, hours_ref, out_ref):
    total = base_ref[...]
    patches = out_ref.shape[0]
    for slot, owner in enumerate(owners(masks, me_ref[0])):
        total += jnp.dot(
            factors_ref[:, pl.ds(pl.multiple_of(owner * patches, patches), patches)],
            hours_ref[slot * patches : (slot + 1) * patches, :],
            preferred_element_type=jnp.float32,
        )
    out_ref[...] = total


def head_kernel(factors_ref, hours_ref, out_ref):
    count = hours_ref.shape[0]
    out_ref[...] = jnp.dot(factors_ref[:, :count], hours_ref[...], preferred_element_type=jnp.float32)


def tail_kernel(start, base_ref, factors_ref, hours_ref, out_ref):
    part = jnp.dot(factors_ref[:, start:], hours_ref[start:, :], preferred_element_type=jnp.float32)
    out_ref[...] = base_ref[...] + part


def sum_kernel(a_ref, b_ref, out_ref):
    out_ref[...] = (a_ref[...] + b_ref[...]).astype(out_ref.dtype)


def shards(size, view_factors, direct_coeff, material, albedo, sky_matrix, sky_order):
    index = lax.axis_index("col").reshape(1)
    rows, hours = sky_matrix.shape
    patches, skies = direct_coeff.shape
    span = size // 2 * rows
    sky, direct_coeff, reflectance, where = call(
        prepare_kernel,
        "prepare",
        (
            pltpu.VMEM(sky_matrix.shape, sky_matrix.dtype),
            pltpu.VMEM(direct_coeff.shape, direct_coeff.dtype),
            pltpu.VMEM((patches, 128), jnp.float32),
            pltpu.VMEM((2, skies), jnp.int32),
        ),
        [ANYWHERE] * 5 + [SCALARS],
        10**9,
        *(pltpu.with_memory_space_constraint(x, pltpu.HBM) for x in (albedo, material, sky_order, sky_matrix, direct_coeff)),
        index,
        scratch=[
            pltpu.SMEM(albedo.shape, albedo.dtype),
            pltpu.VMEM(material.shape, material.dtype),
            pltpu.VMEM(sky_order.shape, sky_order.dtype),
            pltpu.SemaphoreType.DMA((5,)),
        ],
    )
    def permute(masks, name, start=None):
        place = where if start is None else lax.optimization_barrier((where, start))[0]
        return call(
            functools.partial(permute_kernel, masks, rows),
            name,
            (jax.ShapeDtypeStruct((patches, span), jnp.bfloat16),) * 2,
            [SCALARS] + [WHOLE] * 3,
            2 * patches * skies * span,
            index,
            place,
            reflectance,
            direct_coeff,
        )

    order = ("far", "ours", "third", "second", "first", "beside")
    plan, _, _ = gather(size, None, None, None, order, [])
    first = permute(plan.masks, "permute_same")
    late = functools.partial(permute, swap(size, plan, 1).masks, "permute_across")
    same, first, second = gather(size, sky_matrix, sky, sky_matrix, order, first, late, patient=True)
    across = swap(size, same, 1)

    flat = jax.ShapeDtypeStruct((patches, hours), jnp.float32)
    short = jax.ShapeDtypeStruct((patches, hours), jnp.bfloat16)
    flops = 2 * patches * span * hours
    part = call(dot_kernel, "hours_same", flat, [WHOLE] * 2, flops, first[1], same.value)
    own = call(add_dot_kernel, "hours_all", short, [WHOLE] * 3, flops, part, second[1], across.value)
    copy = call(copy_kernel, "copy", pltpu.VMEM(own.shape, own.dtype), [WHOLE], 10**8, own)
    total = call(
        direct_kernel, "direct", flat, [WHOLE] * 4, 2 * 10**9, first[0], second[0], same.value, across.value
    )

    order = ("ours", "beside", "far", "third", "second", "first")
    plan, _, _ = gather(size, None, None, None, order, [])
    factors, _ = lax.optimization_barrier((view_factors, copy))
    chosen = call(
        functools.partial(select_kernel, swap(size, plan, 1).masks),
        "select",
        pltpu.VMEM((patches, size // 2 * patches), view_factors.dtype),
        [SCALARS, WHOLE],
        0,
        index,
        factors,
    )
    theirs = swap(size, Piece(chosen, [[0], [0]]), 1).value
    same, total, _ = gather(size, own, copy, copy, order, total)
    head = same.head.value
    flops = 2 * patches * size // 2 * patches * hours
    partial = call(head_kernel, "partner_head", flat, [WHOLE] * 2, flops, theirs, head)
    partial = call(
        functools.partial(tail_kernel, head.shape[0]), "partner", flat, [WHOLE] * 3, flops, partial, theirs, same.value
    )
    partial = swap(size, Piece(partial, [[0], [0]]), 1).value
    total = call(
        functools.partial(bounce_kernel, same.masks),
        "bounce_same",
        flat,
        [SCALARS] + [WHOLE] * 3,
        flops,
        index,
        total,
        view_factors,
        same.value,
    )
    return call(sum_kernel, "sum", short, [WHOLE] * 2, 0, total, partial)


def solution(mesh):
    return jax.shard_map(
        functools.partial(shards, mesh.shape["col"]),
        mesh=mesh,
        in_specs=(
            P(("parts", "col"), None),
            P(("parts", "col"), None),
            P(("parts", "col")),
            P("parts"),
            P("col", None),
            P(),
        ),
        out_specs=P(("parts", "col"), None),
        check_vma=False,
    )
```

```python
import functools

import jax
import jax.numpy as jnp
from jax import lax
from jax.experimental import pallas as pl
from jax.experimental.pallas import tpu as pltpu
from jax.sharding import PartitionSpec as P

WHOLE = pl.BlockSpec(memory_space=pltpu.VMEM)
ANYWHERE = pl.BlockSpec(memory_space=pltpu.HBM)
SCALARS = pl.BlockSpec(memory_space=pltpu.SMEM)


def parity(i):
    for shift in (8, 4, 2, 1):
        i = i ^ (i >> shift)
    return i & 1


class Piece:
    def __init__(self, value, masks):
        self.value = value
        self.masks = masks


def join(*pieces):
    masks = [sum((p.masks[c] for p in pieces), []) for c in range(2)]
    return Piece(None if pieces[0].value is None else jnp.concatenate([p.value for p in pieces], axis=0), masks)


def swap(size, piece, *bits):
    bits = bits * (2 // len(bits))
    pairs = [(i, i ^ bits[parity(i)]) for i in range(size)]
    masks = [[m ^ bits[c] for m in piece.masks[c ^ parity(bits[c])]] for c in range(2)]
    return Piece(None if piece.value is None else lax.ppermute(piece.value, "col", pairs), masks)


def gather(size, block, copy, sent, order, early, late=None, patient=False):
    exchange = functools.partial(swap, size)
    near, next_, far, *farther = [2 << b | 1 for b in range(size.bit_length() - 2)]
    one, other, both = (near, next_), (next_, near), near ^ next_ ^ 1

    def wait(piece, values):
        if piece.value is not None:
            piece.value, values = lax.optimization_barrier((piece.value, values))
        return values

    block, copy, sent = (Piece(value, [[0], [0]]) for value in (block, copy, sent))
    for bits in farther[::-1]:
        block, copy, sent = (join(piece, exchange(piece, bits)) for piece in (block, copy, sent))
    from_far = exchange(block, far)
    ours = join(copy, exchange(sent, *one))
    beside = exchange(ours, *other)
    early, *_ = wait(from_far, [early, ours.value] if patient else [early])
    third, second, first = exchange(from_far, *other), exchange(from_far, *one), exchange(from_far, both)
    parts = dict(ours=ours, beside=beside, far=from_far, first=first, second=second, third=third)
    if late is not None:
        name, work = late
        late = wait(parts[name], work(parts))
    return join(*(parts[name] for name in order)), early, late


def call(kernel, name, outs, specs, flops, *args, scratch=(), vmem=24):
    return pl.pallas_call(
        kernel,
        scratch_shapes=scratch,
        out_shape=outs,
        in_specs=specs,
        out_specs=jax.tree.map(lambda _: WHOLE, outs),
        compiler_params=pltpu.CompilerParams(vmem_limit_bytes=vmem * 2**20),
        cost_estimate=pl.CostEstimate(flops=flops, bytes_accessed=0, transcendentals=0),
        name=name,
    )(*args)


def prepare_kernel(albedo_in, material_in, order_in, sky_in, direct_in, me_ref, *refs):
    sky_out, direct_out, reflectance_out, where_out, albedo_ref, material_ref, order_ref, sems = refs
    moves = ((albedo_in, albedo_ref), (material_in, material_ref), (order_in, order_ref))
    moves += ((sky_in, sky_out), (direct_in, direct_out))
    copies = [pltpu.make_async_copy(source, target, sems.at[i]) for i, (source, target) in enumerate(moves)]
    for copy in copies:
        copy.start()
    for copy in copies[:3]:
        copy.wait()
    material = material_ref[...].reshape(1, -1)
    reflectance = jnp.zeros(material.shape, jnp.float32)
    for m in range(albedo_ref.shape[0]):
        reflectance = jnp.where(material == m, albedo_ref[m], reflectance)
    reflectance_out[...] = jnp.broadcast_to(reflectance, (128, reflectance.shape[1])).T
    rows = sky_in.shape[0]
    order = order_ref[...].reshape(1, -1)
    owner = (order * -(-(1 << 20) // rows)) >> 20
    where_out[:1] = owner ^ me_ref[0]
    where_out[1:] = order - owner * rows
    for copy in copies[3:]:
        copy.wait()


def permute_kernel(masks, rows, me_ref, where_ref, reflectance_ref, direct_ref, sorted_ref, reflected_ref):
    count = sorted_ref.shape[1]
    odd = parity(me_ref[0])
    apart = where_ref[:1]
    first = jnp.full(apart.shape, -count, jnp.int32)
    for slot, (mask_even, mask_odd) in enumerate(zip(*masks)):
        first = jnp.where(apart == jnp.where(odd == 0, mask_even, mask_odd), slot * rows, first)
    place = first + where_ref[1:]
    reflectance = reflectance_ref[:, :1]
    step = 256
    for j in range(0, count, step):
        width = min(step, count - j)
        position = lax.broadcasted_iota(jnp.int32, (width, place.shape[1]), 0) + j
        pick = jnp.where(position == place, 1.0, 0.0).astype(jnp.bfloat16)
        part = lax.dot_general(direct_ref[...], pick, (((1,), (1,)), ((), ())), preferred_element_type=jnp.float32)
        sorted_ref[:, j : j + width] = part.astype(jnp.bfloat16)
        reflected_ref[:, j : j + width] = (reflectance * part).astype(jnp.bfloat16)


def dot_kernel(a_ref, b_ref, out_ref):
    out_ref[...] = jnp.dot(a_ref[...], b_ref[...], preferred_element_type=jnp.float32)


def add_dot_kernel(base_ref, a_ref, b_ref, out_ref):
    part = jnp.dot(a_ref[...], b_ref[...], preferred_element_type=jnp.float32)
    out_ref[...] = (base_ref[...] + part).astype(out_ref.dtype)


def copy_kernel(in_ref, out_ref):
    out_ref[...] = in_ref[...]


def direct_kernel(first_ref, second_ref, sky_first_ref, sky_second_ref, out_ref):
    out = jnp.dot(first_ref[...], sky_first_ref[...], preferred_element_type=jnp.float32)
    out_ref[...] = out + jnp.dot(second_ref[...], sky_second_ref[...], preferred_element_type=jnp.float32)


def owners(masks, me):
    odd = parity(me)
    return [me ^ jnp.where(odd == 0, mask_even, mask_odd) for mask_even, mask_odd in zip(*masks)]


def select_kernel(masks, me_ref, factors_ref, out_ref):
    patches = out_ref.shape[0]
    for slot, owner in enumerate(owners(masks, me_ref[0])):
        columns = factors_ref[:, pl.ds(pl.multiple_of(owner * patches, patches), patches)]
        out_ref[:, slot * patches : (slot + 1) * patches] = columns


def bounce_kernel(masks, me_ref, base_ref, factors_ref, hours_ref, out_ref):
    total = base_ref[...]
    patches = out_ref.shape[0]
    for slot, owner in enumerate(owners(masks, me_ref[0])):
        total += jnp.dot(
            factors_ref[:, pl.ds(pl.multiple_of(owner * patches, patches), patches)],
            hours_ref[slot * patches : (slot + 1) * patches, :],
            preferred_element_type=jnp.float32,
        )
    out_ref[...] = total


def head_kernel(factors_ref, hours_ref, out_ref):
    count = hours_ref.shape[0]
    out_ref[...] = jnp.dot(factors_ref[:, :count], hours_ref[...], preferred_element_type=jnp.float32)


def tail_kernel(start, base_ref, factors_ref, hours_ref, out_ref):
    part = jnp.dot(factors_ref[:, start:], hours_ref[start:, :], preferred_element_type=jnp.float32)
    out_ref[...] = base_ref[...] + part


def sum_kernel(a_ref, b_ref, out_ref):
    out_ref[...] = (a_ref[...] + b_ref[...]).astype(out_ref.dtype)


def shards(size, view_factors, direct_coeff, material, albedo, sky_matrix, sky_order):
    index = lax.axis_index("col").reshape(1)
    rows, hours = sky_matrix.shape
    patches, skies = direct_coeff.shape
    span = size // 2 * rows
    sky, direct_coeff, reflectance, where = call(
        prepare_kernel,
        "prepare",
        (
            pltpu.VMEM(sky_matrix.shape, sky_matrix.dtype),
            pltpu.VMEM(direct_coeff.shape, direct_coeff.dtype),
            pltpu.VMEM((patches, 128), jnp.float32),
            pltpu.VMEM((2, skies), jnp.int32),
        ),
        [ANYWHERE] * 5 + [SCALARS],
        10**9,
        *(pltpu.with_memory_space_constraint(x, pltpu.HBM) for x in (albedo, material, sky_order, sky_matrix, direct_coeff)),
        index,
        scratch=[
            pltpu.SMEM(albedo.shape, albedo.dtype),
            pltpu.VMEM(material.shape, material.dtype),
            pltpu.VMEM(sky_order.shape, sky_order.dtype),
            pltpu.SemaphoreType.DMA((5,)),
        ],
    )
    def permute(masks, name, start=None):
        place = where if start is None else lax.optimization_barrier((where, start))[0]
        return call(
            functools.partial(permute_kernel, masks, rows),
            name,
            (jax.ShapeDtypeStruct((patches, span), jnp.bfloat16),) * 2,
            [SCALARS] + [WHOLE] * 3,
            2 * patches * skies * span,
            index,
            place,
            reflectance,
            direct_coeff,
        )

    order = ("far", "ours", "third", "second", "first", "beside")
    plan, _, _ = gather(size, None, None, None, order, [])
    first = permute(plan.masks, "permute_same")
    masks = swap(size, plan, 1).masks
    late = ("first", lambda parts: permute(masks, "permute_across", parts["far"].value))
    same, first, second = gather(size, sky_matrix, sky, sky_matrix, order, first, late, patient=True)
    across = swap(size, same, 1)

    flat = jax.ShapeDtypeStruct((patches, hours), jnp.float32)
    short = jax.ShapeDtypeStruct((patches, hours), jnp.bfloat16)
    flops = 2 * patches * span * hours
    part = call(dot_kernel, "hours_same", flat, [WHOLE] * 2, flops, first[1], same.value)
    own = call(add_dot_kernel, "hours_all", short, [WHOLE] * 3, flops, part, second[1], across.value)
    copy = call(copy_kernel, "copy", pltpu.VMEM(own.shape, own.dtype), [WHOLE], 10**8, own)
    total = call(
        direct_kernel, "direct", flat, [WHOLE] * 4, 2 * 10**9, first[0], second[0], same.value, across.value
    )

    order = ("ours", "beside", "far", "third", "second", "first")
    plan, _, _ = gather(size, None, None, None, order, [])
    factors, _ = lax.optimization_barrier((view_factors, copy))
    chosen = call(
        functools.partial(select_kernel, swap(size, plan, 1).masks),
        "select",
        pltpu.VMEM((patches, size // 2 * patches), view_factors.dtype),
        [SCALARS, WHOLE],
        0,
        index,
        factors,
    )
    theirs = swap(size, Piece(chosen, [[0], [0]]), 1).value
    flops = 2 * patches * size // 2 * patches * hours
    head = []

    def partner_head(parts):
        head.append(join(*(parts[name] for name in order[:3])))
        return call(head_kernel, "partner_head", flat, [WHOLE] * 2, 2 * 10**9, theirs, head[0].value)

    same, total, partial = gather(size, own, copy, copy, order, total, ("second", partner_head))
    start = head[0].value.shape[0]
    partial = call(
        functools.partial(tail_kernel, start), "partner", flat, [WHOLE] * 3, flops, partial, theirs, same.value
    )
    partial = swap(size, Piece(partial, [[0], [0]]), 1).value
    total = call(
        functools.partial(bounce_kernel, same.masks),
        "bounce_same",
        flat,
        [SCALARS] + [WHOLE] * 3,
        flops,
        index,
        total,
        view_factors,
        same.value,
    )
    return call(sum_kernel, "sum", short, [WHOLE] * 2, 0, total, partial)


def solution(mesh):
    return jax.shard_map(
        functools.partial(shards, mesh.shape["col"]),
        mesh=mesh,
        in_specs=(
            P(("parts", "col"), None),
            P(("parts", "col"), None),
            P(("parts", "col")),
            P("parts"),
            P("col", None),
            P(),
        ),
        out_specs=P(("parts", "col"), None),
        check_vma=False,
    )
```

```python
import functools

import jax
import jax.numpy as jnp
from jax import lax
from jax.experimental import pallas as pl
from jax.experimental.pallas import tpu as pltpu
from jax.sharding import PartitionSpec as P

WHOLE = pl.BlockSpec(memory_space=pltpu.VMEM)
ANYWHERE = pl.BlockSpec(memory_space=pltpu.HBM)
SCALARS = pl.BlockSpec(memory_space=pltpu.SMEM)


def parity(i):
    for shift in (8, 4, 2, 1):
        i = i ^ (i >> shift)
    return i & 1


class Piece:
    def __init__(self, value, masks):
        self.value = value
        self.masks = masks


def join(*pieces):
    masks = [sum((p.masks[c] for p in pieces), []) for c in range(2)]
    return Piece(None if pieces[0].value is None else jnp.concatenate([p.value for p in pieces], axis=0), masks)


def swap(size, piece, *bits):
    bits = bits * (2 // len(bits))
    pairs = [(i, i ^ bits[parity(i)]) for i in range(size)]
    masks = [[m ^ bits[c] for m in piece.masks[c ^ parity(bits[c])]] for c in range(2)]
    return Piece(None if piece.value is None else lax.ppermute(piece.value, "col", pairs), masks)


def gather(size, block, copy, sent, order, early, late=None, patient=False):
    exchange = functools.partial(swap, size)
    near, next_, far, *farther = [2 << b | 1 for b in range(size.bit_length() - 2)]
    one, other, both = (near, next_), (next_, near), near ^ next_ ^ 1

    def wait(piece, values):
        if piece.value is not None:
            piece.value, values = lax.optimization_barrier((piece.value, values))
        return values

    block, copy, sent = (Piece(value, [[0], [0]]) for value in (block, copy, sent))
    for bits in farther[::-1]:
        block, copy, sent = (join(piece, exchange(piece, bits)) for piece in (block, copy, sent))
    from_far = exchange(block, far)
    ours = join(copy, exchange(sent, *one))
    beside = exchange(ours, *other)
    early, *_ = wait(from_far, [early, ours.value] if patient else [early])
    third, second, first = exchange(from_far, *other), exchange(from_far, *one), exchange(from_far, both)
    parts = dict(ours=ours, beside=beside, far=from_far, first=first, second=second, third=third)
    if late is not None:
        name, work = late
        late = wait(parts[name], work(parts))
    return join(*(parts[name] for name in order)), early, late


def call(kernel, name, outs, specs, flops, *args, scratch=(), vmem=24):
    return pl.pallas_call(
        kernel,
        scratch_shapes=scratch,
        out_shape=outs,
        in_specs=specs,
        out_specs=jax.tree.map(lambda _: WHOLE, outs),
        compiler_params=pltpu.CompilerParams(vmem_limit_bytes=vmem * 2**20),
        cost_estimate=pl.CostEstimate(flops=flops, bytes_accessed=0, transcendentals=0),
        name=name,
    )(*args)


def prepare_kernel(albedo_in, material_in, order_in, sky_in, direct_in, me_ref, *refs):
    sky_out, direct_out, reflectance_out, where_out, albedo_ref, material_ref, order_ref, sems = refs
    moves = ((albedo_in, albedo_ref), (material_in, material_ref), (order_in, order_ref))
    moves += ((sky_in, sky_out), (direct_in, direct_out))
    copies = [pltpu.make_async_copy(source, target, sems.at[i]) for i, (source, target) in enumerate(moves)]
    for copy in copies:
        copy.start()
    for copy in copies[:3]:
        copy.wait()
    material = material_ref[...].reshape(1, -1)
    reflectance = jnp.zeros(material.shape, jnp.float32)
    for m in range(albedo_ref.shape[0]):
        reflectance = jnp.where(material == m, albedo_ref[m], reflectance)
    reflectance_out[...] = jnp.broadcast_to(reflectance, (128, reflectance.shape[1])).T
    rows = sky_in.shape[0]
    order = order_ref[...].reshape(1, -1)
    owner = (order * -(-(1 << 20) // rows)) >> 20
    where_out[:1] = owner ^ me_ref[0]
    where_out[1:] = order - owner * rows
    for copy in copies[3:]:
        copy.wait()


def permute_kernel(masks, rows, me_ref, where_ref, reflectance_ref, direct_ref, sorted_ref, reflected_ref):
    count = sorted_ref.shape[1]
    odd = parity(me_ref[0])
    apart = where_ref[:1]
    first = jnp.full(apart.shape, -count, jnp.int32)
    for slot, (mask_even, mask_odd) in enumerate(zip(*masks)):
        first = jnp.where(apart == jnp.where(odd == 0, mask_even, mask_odd), slot * rows, first)
    place = first + where_ref[1:]
    reflectance = reflectance_ref[:, :1]
    step = 256
    for j in range(0, count, step):
        width = min(step, count - j)
        position = lax.broadcasted_iota(jnp.int32, (width, place.shape[1]), 0) + j
        pick = jnp.where(position == place, 1.0, 0.0).astype(jnp.bfloat16)
        part = lax.dot_general(direct_ref[...], pick, (((1,), (1,)), ((), ())), preferred_element_type=jnp.float32)
        sorted_ref[:, j : j + width] = part.astype(jnp.bfloat16)
        reflected_ref[:, j : j + width] = (reflectance * part).astype(jnp.bfloat16)


def dot_kernel(a_ref, b_ref, out_ref):
    out_ref[...] = jnp.dot(a_ref[...], b_ref[...], preferred_element_type=jnp.float32)


def add_dot_kernel(base_ref, a_ref, b_ref, out_ref):
    part = jnp.dot(a_ref[...], b_ref[...], preferred_element_type=jnp.float32)
    out_ref[...] = (base_ref[...] + part).astype(out_ref.dtype)


def copy_kernel(in_ref, out_ref):
    out_ref[...] = in_ref[...]


def direct_kernel(first_ref, second_ref, sky_first_ref, sky_second_ref, out_ref):
    out = jnp.dot(first_ref[...], sky_first_ref[...], preferred_element_type=jnp.float32)
    out_ref[...] = out + jnp.dot(second_ref[...], sky_second_ref[...], preferred_element_type=jnp.float32)


def owners(masks, me):
    odd = parity(me)
    return [me ^ jnp.where(odd == 0, mask_even, mask_odd) for mask_even, mask_odd in zip(*masks)]


def select_kernel(masks, me_ref, factors_ref, out_ref):
    patches = out_ref.shape[0]
    for slot, owner in enumerate(owners(masks, me_ref[0])):
        columns = factors_ref[:, pl.ds(pl.multiple_of(owner * patches, patches), patches)]
        out_ref[:, slot * patches : (slot + 1) * patches] = columns


def bounce_kernel(masks, me_ref, base_ref, factors_ref, hours_ref, out_ref):
    total = base_ref[...]
    patches = out_ref.shape[0]
    for slot, owner in enumerate(owners(masks, me_ref[0])):
        total += jnp.dot(
            factors_ref[:, pl.ds(pl.multiple_of(owner * patches, patches), patches)],
            hours_ref[slot * patches : (slot + 1) * patches, :],
            preferred_element_type=jnp.float32,
        )
    out_ref[...] = total


def head_kernel(factors_ref, hours_ref, out_ref):
    count = hours_ref.shape[0]
    out_ref[...] = jnp.dot(factors_ref[:, :count], hours_ref[...], preferred_element_type=jnp.float32)


def tail_kernel(start, base_ref, factors_ref, hours_ref, out_ref):
    part = jnp.dot(factors_ref[:, start:], hours_ref[start:, :], preferred_element_type=jnp.float32)
    out_ref[...] = (base_ref[...] + part).astype(out_ref.dtype)


def sum_kernel(a_ref, b_ref, out_ref):
    out_ref[...] = (a_ref[...] + b_ref[...]).astype(out_ref.dtype)


def shards(size, view_factors, direct_coeff, material, albedo, sky_matrix, sky_order):
    index = lax.axis_index("col").reshape(1)
    rows, hours = sky_matrix.shape
    patches, skies = direct_coeff.shape
    span = size // 2 * rows
    sky, direct_coeff, reflectance, where = call(
        prepare_kernel,
        "prepare",
        (
            pltpu.VMEM(sky_matrix.shape, sky_matrix.dtype),
            pltpu.VMEM(direct_coeff.shape, direct_coeff.dtype),
            pltpu.VMEM((patches, 128), jnp.float32),
            pltpu.VMEM((2, skies), jnp.int32),
        ),
        [ANYWHERE] * 5 + [SCALARS],
        10**9,
        *(pltpu.with_memory_space_constraint(x, pltpu.HBM) for x in (albedo, material, sky_order, sky_matrix, direct_coeff)),
        index,
        scratch=[
            pltpu.SMEM(albedo.shape, albedo.dtype),
            pltpu.VMEM(material.shape, material.dtype),
            pltpu.VMEM(sky_order.shape, sky_order.dtype),
            pltpu.SemaphoreType.DMA((5,)),
        ],
    )
    def permute(masks, name, start=None):
        place = where if start is None else lax.optimization_barrier((where, start))[0]
        return call(
            functools.partial(permute_kernel, masks, rows),
            name,
            (jax.ShapeDtypeStruct((patches, span), jnp.bfloat16),) * 2,
            [SCALARS] + [WHOLE] * 3,
            2 * patches * skies * span,
            index,
            place,
            reflectance,
            direct_coeff,
        )

    order = ("far", "ours", "third", "second", "first", "beside")
    plan, _, _ = gather(size, None, None, None, order, [])
    first = permute(plan.masks, "permute_same")
    masks = swap(size, plan, 1).masks
    late = ("first", lambda parts: permute(masks, "permute_across", parts["far"].value))
    same, first, second = gather(size, sky_matrix, sky, sky_matrix, order, first, late, patient=True)
    across = swap(size, same, 1)

    flat = jax.ShapeDtypeStruct((patches, hours), jnp.float32)
    short = jax.ShapeDtypeStruct((patches, hours), jnp.bfloat16)
    flops = 2 * patches * span * hours
    part = call(dot_kernel, "hours_same", flat, [WHOLE] * 2, flops, first[1], same.value)
    own = call(add_dot_kernel, "hours_all", short, [WHOLE] * 3, flops, part, second[1], across.value)
    copy = call(copy_kernel, "copy", pltpu.VMEM(own.shape, own.dtype), [WHOLE], 10**8, own)
    total = call(
        direct_kernel, "direct", flat, [WHOLE] * 4, 2 * 10**9, first[0], second[0], same.value, across.value
    )

    order = ("ours", "beside", "far", "third", "second", "first")
    plan, _, _ = gather(size, None, None, None, order, [])
    factors, _ = lax.optimization_barrier((view_factors, copy))
    chosen = call(
        functools.partial(select_kernel, swap(size, plan, 1).masks),
        "select",
        pltpu.VMEM((patches, size // 2 * patches), view_factors.dtype),
        [SCALARS, WHOLE],
        0,
        index,
        factors,
    )
    theirs = swap(size, Piece(chosen, [[0], [0]]), 1).value
    flops = 2 * patches * size // 2 * patches * hours
    head = []

    def partner_head(parts):
        head.append(join(*(parts[name] for name in order[:3])))
        return call(head_kernel, "partner_head", flat, [WHOLE] * 2, 2 * 10**9, theirs, head[0].value)

    same, total, partial = gather(size, own, copy, copy, order, total, ("second", partner_head))
    start = head[0].value.shape[0]
    partial = call(
        functools.partial(tail_kernel, start), "partner", short, [WHOLE] * 3, flops, partial, theirs, same.value
    )
    partial = swap(size, Piece(partial, [[0], [0]]), 1).value
    total = call(
        functools.partial(bounce_kernel, same.masks),
        "bounce_same",
        flat,
        [SCALARS] + [WHOLE] * 3,
        flops,
        index,
        total,
        view_factors,
        same.value,
    )
    return call(sum_kernel, "sum", short, [WHOLE] * 2, 0, total, partial)


def solution(mesh):
    return jax.shard_map(
        functools.partial(shards, mesh.shape["col"]),
        mesh=mesh,
        in_specs=(
            P(("parts", "col"), None),
            P(("parts", "col"), None),
            P(("parts", "col")),
            P("parts"),
            P("col", None),
            P(),
        ),
        out_specs=P(("parts", "col"), None),
        check_vma=False,
    )
```

```python
import functools

import jax
import jax.numpy as jnp
from jax import lax
from jax.experimental import pallas as pl
from jax.experimental.pallas import tpu as pltpu
from jax.sharding import PartitionSpec as P

WHOLE = pl.BlockSpec(memory_space=pltpu.VMEM)
ANYWHERE = pl.BlockSpec(memory_space=pltpu.HBM)
SCALARS = pl.BlockSpec(memory_space=pltpu.SMEM)


def parity(i):
    for shift in (8, 4, 2, 1):
        i = i ^ (i >> shift)
    return i & 1


class Piece:
    def __init__(self, value, masks):
        self.value = value
        self.masks = masks


def join(*pieces):
    masks = [sum((p.masks[c] for p in pieces), []) for c in range(2)]
    return Piece(None if pieces[0].value is None else jnp.concatenate([p.value for p in pieces], axis=0), masks)


def swap(size, piece, *bits):
    bits = bits * (2 // len(bits))
    pairs = [(i, i ^ bits[parity(i)]) for i in range(size)]
    masks = [[m ^ bits[c] for m in piece.masks[c ^ parity(bits[c])]] for c in range(2)]
    return Piece(None if piece.value is None else lax.ppermute(piece.value, "col", pairs), masks)


def gather(size, block, copy, sent, order, early, late=None, patient=False):
    exchange = functools.partial(swap, size)
    near, next_, far, *farther = [2 << b | 1 for b in range(size.bit_length() - 2)]
    one, other, both = (near, next_), (next_, near), near ^ next_ ^ 1

    def wait(piece, values):
        if piece.value is not None:
            piece.value, values = lax.optimization_barrier((piece.value, values))
        return values

    block, copy, sent = (Piece(value, [[0], [0]]) for value in (block, copy, sent))
    for bits in farther[::-1]:
        block, copy, sent = (join(piece, exchange(piece, bits)) for piece in (block, copy, sent))
    from_far = exchange(block, far)
    ours = join(copy, exchange(sent, *one))
    beside = exchange(ours, *other)
    early, *_ = wait(from_far, [early, ours.value] if patient else [early])
    third, second, first = exchange(from_far, *other), exchange(from_far, *one), exchange(from_far, both)
    parts = dict(ours=ours, beside=beside, far=from_far, first=first, second=second, third=third)
    if late is not None:
        name, work = late
        late = wait(parts[name], work(parts))
    return join(*(parts[name] for name in order)), early, late


def call(kernel, name, outs, specs, flops, *args, scratch=(), vmem=24):
    return pl.pallas_call(
        kernel,
        scratch_shapes=scratch,
        out_shape=outs,
        in_specs=specs,
        out_specs=jax.tree.map(lambda _: WHOLE, outs),
        compiler_params=pltpu.CompilerParams(vmem_limit_bytes=vmem * 2**20),
        cost_estimate=pl.CostEstimate(flops=flops, bytes_accessed=0, transcendentals=0),
        name=name,
    )(*args)


def prepare_kernel(albedo_in, material_in, order_in, sky_in, direct_in, me_ref, *refs):
    sky_out, direct_out, reflectance_out, where_out, albedo_ref, material_ref, order_ref, sems = refs
    moves = ((albedo_in, albedo_ref), (material_in, material_ref), (order_in, order_ref))
    moves += ((sky_in, sky_out), (direct_in, direct_out))
    copies = [pltpu.make_async_copy(source, target, sems.at[i]) for i, (source, target) in enumerate(moves)]
    for copy in copies:
        copy.start()
    for copy in copies[:3]:
        copy.wait()
    material = material_ref[...].reshape(1, -1)
    reflectance = jnp.zeros(material.shape, jnp.float32)
    for m in range(albedo_ref.shape[0]):
        reflectance = jnp.where(material == m, albedo_ref[m], reflectance)
    reflectance_out[...] = jnp.broadcast_to(reflectance, (128, reflectance.shape[1])).T
    rows = sky_in.shape[0]
    order = order_ref[...].reshape(1, -1)
    owner = (order * -(-(1 << 20) // rows)) >> 20
    where_out[:1] = owner ^ me_ref[0]
    where_out[1:] = order - owner * rows
    for copy in copies[3:]:
        copy.wait()


def permute_kernel(masks, rows, me_ref, where_ref, reflectance_ref, direct_ref, sorted_ref, reflected_ref):
    count = sorted_ref.shape[1]
    odd = parity(me_ref[0])
    apart = where_ref[:1]
    first = jnp.full(apart.shape, -count, jnp.int32)
    for slot, (mask_even, mask_odd) in enumerate(zip(*masks)):
        first = jnp.where(apart == jnp.where(odd == 0, mask_even, mask_odd), slot * rows, first)
    place = first + where_ref[1:]
    reflectance = reflectance_ref[:, :1]
    step = 256
    for j in range(0, count, step):
        width = min(step, count - j)
        position = lax.broadcasted_iota(jnp.int32, (width, place.shape[1]), 0) + j
        pick = jnp.where(position == place, 1.0, 0.0).astype(jnp.bfloat16)
        part = lax.dot_general(direct_ref[...], pick, (((1,), (1,)), ((), ())), preferred_element_type=jnp.float32)
        sorted_ref[:, j : j + width] = part.astype(jnp.bfloat16)
        reflected_ref[:, j : j + width] = (reflectance * part).astype(jnp.bfloat16)


def dot_kernel(a_ref, b_ref, out_ref):
    out_ref[...] = jnp.dot(a_ref[...], b_ref[...], preferred_element_type=jnp.float32).astype(out_ref.dtype)


def add_dot_kernel(base_ref, a_ref, b_ref, out_ref):
    part = jnp.dot(a_ref[...], b_ref[...], preferred_element_type=jnp.float32)
    out_ref[...] = (base_ref[...] + part).astype(out_ref.dtype)


def copy_kernel(in_ref, out_ref):
    out_ref[...] = in_ref[...]


def direct_kernel(first_ref, second_ref, sky_first_ref, sky_second_ref, out_ref):
    out = jnp.dot(first_ref[...], sky_first_ref[...], preferred_element_type=jnp.float32)
    out_ref[...] = out + jnp.dot(second_ref[...], sky_second_ref[...], preferred_element_type=jnp.float32)


def owners(masks, me):
    odd = parity(me)
    return [me ^ jnp.where(odd == 0, mask_even, mask_odd) for mask_even, mask_odd in zip(*masks)]


def select_kernel(masks, me_ref, factors_ref, out_ref):
    patches = out_ref.shape[0]
    for slot, owner in enumerate(owners(masks, me_ref[0])):
        columns = factors_ref[:, pl.ds(pl.multiple_of(owner * patches, patches), patches)]
        out_ref[:, slot * patches : (slot + 1) * patches] = columns


def bounce_kernel(masks, me_ref, base_ref, factors_ref, hours_ref, out_ref):
    total = base_ref[...]
    patches = out_ref.shape[0]
    start = hours_ref.shape[0] // patches - len(masks[0])
    for slot, owner in enumerate(owners(masks, me_ref[0]), start):
        total += jnp.dot(
            factors_ref[:, pl.ds(pl.multiple_of(owner * patches, patches), patches)],
            hours_ref[slot * patches : (slot + 1) * patches, :],
            preferred_element_type=jnp.float32,
        )
    out_ref[...] = total


def sum_kernel(a_ref, b_ref, out_ref):
    out_ref[...] = (a_ref[...] + b_ref[...]).astype(out_ref.dtype)


def shards(size, view_factors, direct_coeff, material, albedo, sky_matrix, sky_order):
    index = lax.axis_index("col").reshape(1)
    rows, hours = sky_matrix.shape
    patches, skies = direct_coeff.shape
    span = size // 2 * rows
    sky, direct_coeff, reflectance, where = call(
        prepare_kernel,
        "prepare",
        (
            pltpu.VMEM(sky_matrix.shape, sky_matrix.dtype),
            pltpu.VMEM(direct_coeff.shape, direct_coeff.dtype),
            pltpu.VMEM((patches, 128), jnp.float32),
            pltpu.VMEM((2, skies), jnp.int32),
        ),
        [ANYWHERE] * 5 + [SCALARS],
        10**9,
        *(pltpu.with_memory_space_constraint(x, pltpu.HBM) for x in (albedo, material, sky_order, sky_matrix, direct_coeff)),
        index,
        scratch=[
            pltpu.SMEM(albedo.shape, albedo.dtype),
            pltpu.VMEM(material.shape, material.dtype),
            pltpu.VMEM(sky_order.shape, sky_order.dtype),
            pltpu.SemaphoreType.DMA((5,)),
        ],
    )
    def permute(masks, name, start=None):
        place = where if start is None else lax.optimization_barrier((where, start))[0]
        return call(
            functools.partial(permute_kernel, masks, rows),
            name,
            (jax.ShapeDtypeStruct((patches, span), jnp.bfloat16),) * 2,
            [SCALARS] + [WHOLE] * 3,
            2 * patches * skies * span,
            index,
            place,
            reflectance,
            direct_coeff,
        )

    order = ("far", "ours", "third", "second", "first", "beside")
    plan, _, _ = gather(size, None, None, None, order, [])
    first = permute(plan.masks, "permute_same")
    masks = swap(size, plan, 1).masks
    late = ("first", lambda parts: permute(masks, "permute_across", parts["far"].value))
    same, first, second = gather(size, sky_matrix, sky, sky_matrix, order, first, late, patient=True)
    across = swap(size, same, 1)

    flat = jax.ShapeDtypeStruct((patches, hours), jnp.float32)
    short = jax.ShapeDtypeStruct((patches, hours), jnp.bfloat16)
    flops = 2 * patches * span * hours
    part = call(dot_kernel, "hours_same", flat, [WHOLE] * 2, flops, first[1], same.value)
    own = call(add_dot_kernel, "hours_all", short, [WHOLE] * 3, flops, part, second[1], across.value)
    copy = call(copy_kernel, "copy", pltpu.VMEM(own.shape, own.dtype), [WHOLE], 10**8, own)
    total = call(
        direct_kernel, "direct", flat, [WHOLE] * 4, 2 * 10**9, first[0], second[0], same.value, across.value
    )

    order = ("ours", "beside", "far", "third", "second", "first")
    plan, _, _ = gather(size, None, None, None, order, [])
    factors, _ = lax.optimization_barrier((view_factors, copy))
    chosen = call(
        functools.partial(select_kernel, swap(size, plan, 1).masks),
        "select",
        pltpu.VMEM((patches, size // 2 * patches), view_factors.dtype),
        [SCALARS, WHOLE],
        0,
        index,
        factors,
    )
    theirs = swap(size, Piece(chosen, [[0], [0]]), 1).value
    flops = 2 * patches * size // 2 * patches * hours
    done = []

    def bounce(name, base, piece):
        masks = [m[len(done) :] for m in piece.masks]
        done.extend(masks[0])
        args = (index, base, view_factors, piece.value)
        return call(functools.partial(bounce_kernel, masks), name, flat, [SCALARS] + [WHOLE] * 3, 2 * 10**9, *args)

    late = ("first", lambda parts: bounce("bounce_head", total, join(*(parts[name] for name in order[:2]))))
    same, _, total = gather(size, own, copy, copy, order, total, late)
    partial = call(dot_kernel, "partner", short, [WHOLE] * 2, flops, theirs, same.value)
    partial = swap(size, Piece(partial, [[0], [0]]), 1).value
    total = bounce("bounce_same", total, same)
    return call(sum_kernel, "sum", short, [WHOLE] * 2, 0, total, partial)


def solution(mesh):
    return jax.shard_map(
        functools.partial(shards, mesh.shape["col"]),
        mesh=mesh,
        in_specs=(
            P(("parts", "col"), None),
            P(("parts", "col"), None),
            P(("parts", "col")),
            P("parts"),
            P("col", None),
            P(),
        ),
        out_specs=P(("parts", "col"), None),
        check_vma=False,
    )
```
